32 devices in a mesh: dp: 16 (over z, y, core), seq: 2 (over x).
Axes of the slice: x: 2, y: 2, z: 4, core: 2. Of those that a mesh axis runs over, the one named last changes fastest.
Arguments:
- tokens: bfloat16 [16384, 1024], P(('dp', 'seq')), may hold values from -6 to 6
- gain_in: bfloat16 [1024], P(('dp', 'seq')), may hold values from 0.5 to 1.5
- w_query: bfloat16 [1024, 512], P(('dp', 'seq')), may hold values from -0.1875 to 0.1875
- key_projection: bfloat16 [1024, 128], P(('dp', 'seq')), may hold values from -0.1875 to 0.1875
- value_projection: bfloat16 [1024, 128], P(('dp', 'seq')), may hold values from -0.1875 to 0.1875
- w_output: bfloat16 [1024, 512], P(('dp', 'seq')), may hold values from -2 to 2
- w_zgate: bfloat16 [1024, 1536], P(('dp', 'seq')), may hold values from -0.1875 to 0.1875
- w_inner: bfloat16 [1024, 1792], P(('dp', 'seq')), may hold values from -0.1875 to 0.1875
- w_step: bfloat16 [1024, 24], P(('dp', 'seq')), may hold values from -0.1875 to 0.1875
- conv_taps: bfloat16 [4, 1792], P(None, ('dp', 'seq')), may hold values from -3 to 3
- conv_bias: bfloat16 [1792], P(('dp', 'seq')), may hold values from -3 to 3
- ssm_gain: bfloat16 [1536], P(('dp', 'seq')), may hold values from 0.5 to 1.5
- w_mixout: bfloat16 [1024, 1536], P(('dp', 'seq')), may hold values from -0.15625 to 0.15625
- gain_mlp: bfloat16 [1024], P(('dp', 'seq')), may hold values from 0.5 to 1.5
- w_gate: bfloat16 [1024, 2048], P(('dp', 'seq')), may hold values from -0.1875 to 0.1875
- w_up: bfloat16 [1024, 2048], P(('dp', 'seq')), may hold values from -0.1875 to 0.1875
- w_down: bfloat16 [1024, 2048], P(('dp', 'seq')), may hold values from -0.125 to 0.125
- head_params: float32 [3, 24], replicated, may hold values from -10 to 1.5, as said below
- cotangent: bfloat16 [16384, 1024], P(('dp', 'seq')), may hold values from -6 to 6
Outputs:
- output: bfloat16 [16384, 1024], P(('dp', 'seq'))
- grad_tokens: bfloat16 [16384, 1024], P(('dp', 'seq'))
- grad_gain_in: float32 [1024], P(('dp', 'seq'))
- grad_w_query: float32 [1024, 512], P(('dp', 'seq'))
- grad_w_key: float32 [1024, 128], P(('dp', 'seq'))
- grad_w_value: float32 [1024, 128], P(('dp', 'seq'))
- grad_w_output: float32 [1024, 512], P(('dp', 'seq'))
- grad_w_zgate: float32 [1024, 1536], P(('dp', 'seq'))
- grad_w_inner: float32 [1024, 1792], P(('dp', 'seq'))
- grad_w_step: float32 [1024, 24], P(('dp', 'seq'))
- grad_conv_taps: float32 [4, 1792], P(None, ('dp', 'seq'))
- grad_conv_bias: float32 [1792], P(('dp', 'seq'))
- grad_ssm_gain: float32 [1536], P(('dp', 'seq'))
- grad_w_mixout: float32 [1024, 1536], P(('dp', 'seq'))
- grad_gain_mlp: float32 [1024], P(('dp', 'seq'))
- grad_w_gate: float32 [1024, 2048], P(('dp', 'seq'))
- grad_w_up: float32 [1024, 2048], P(('dp', 'seq'))
- grad_w_down: float32 [1024, 2048], P(('dp', 'seq'))
- grad_head: float32 [3, 24], replicated
The draws below stay inside these ranges and needn't reach their ends.
Inputs may be any that keep to these rules, and one draw needn't show every extreme that they name: `head_params`: row 0 holds the heads' step biases, row 1 the logarithms of their rates, row 2 their skip gains.
All inputs are finite; a program needn't handle non-finite values.
Results may differ from the reference program's by a relative error of at most 0.014.
Values may be sent and summed in bfloat16 or wider, within the bound.
A program may use at most 256 MiB of HBM per device.

```python
import math
import jax
import jax.numpy as jnp
from jax import lax

MODEL_WIDTH = 1024
QUERY_HEADS = 8
KEY_VALUE_HEADS = 2
HEAD_SIZE = 64
H = 24
N = 128
KW = 4
FF = 2048
SEQ_LEN = 1024
DSSM = 1536
CONV = 1792
TOKENS = 16384


def draw_head_params(key, part):
    key = jax.random.fold_in(key, 11)
    subkeys = jax.random.split(key, 3)
    spread = jax.random.uniform(subkeys[0], (H,), jnp.float32)
    step_bias = -3.0 - spread * (math.log(SEQ_LEN) - 2.5)
    log_rate = 0.7 * jax.random.uniform(subkeys[1], (H,), jnp.float32)
    skip_gain = 0.5 + jax.random.uniform(subkeys[2], (H,), jnp.float32)
    return jnp.stack([step_bias, log_rate, skip_gain])


def strengthened(drawn, own_key, source, target, blocks, factor):
    owner, partner = [(jnp.arange(drawn.shape[axis_at]) // (drawn.shape[axis_at] // blocks)).reshape([-1 if axis == axis_at else 1 for axis in range(drawn.ndim)]) for axis_at in (source, target)]
    chosen = jax.random.permutation(own_key, blocks)[partner]
    strong = (owner == chosen) | (owner == (partner + blocks // 2) % blocks)
    return jnp.where(strong, factor * drawn, drawn)


def levels(key, extent, cuts, least, top_value):
    gain, own = 1.0, jax.random.fold_in(key, 6)
    for dim, shards_of in cuts:
        draws = jnp.exp(jax.random.uniform(jax.random.fold_in(own, dim), (shards_of,), jnp.float32, least / len(cuts), top_value / len(cuts)))
        gain = gain * jnp.repeat(draws, extent[dim] // shards_of).reshape([-1 if axis == dim else 1 for axis in range(len(extent))])
    return gain


def scatter_about(stream_key, extent, scale, limit, cuts=(), held_as=jnp.bfloat16):
    array = scale * jax.random.normal(stream_key, extent, jnp.float32)
    if cuts:
        array = array * levels(stream_key, extent, cuts, -0.22, 0.18)
    return jnp.clip(array, -limit, limit).astype(held_as)


def noise_with(key, dims, width, reach, shards, heavy, kind=jnp.bfloat16):
    result = width * jax.random.normal(key, dims, jnp.float32)
    if shards:
        result = result * levels(key, dims, shards, -0.22, 0.18)
    return jnp.clip(strengthened(result, jax.random.fold_in(key, 3), *heavy), -reach, reach).astype(kind)


def setup_inputs(seed: int = 0) -> dict:
    key_list = jax.random.split(jax.random.key(seed), 20)
    return {
        "tokens": noise_with(key_list[0], (TOKENS, MODEL_WIDTH), 1.0, 6.0, ((0, 32),), (0, 1, 32, 2.75)),
        "gain_in": jnp.clip(1.0 + 0.1 * jax.random.normal(key_list[1], (MODEL_WIDTH,), jnp.float32), 0.5, 1.5).astype(jnp.bfloat16),
        "w_query": scatter_about(key_list[2], (MODEL_WIDTH, QUERY_HEADS * HEAD_SIZE), MODEL_WIDTH ** -0.5, 0.1875, ((0, 32),)),
        "key_projection": scatter_about(key_list[3], (MODEL_WIDTH, KEY_VALUE_HEADS * HEAD_SIZE), MODEL_WIDTH ** -0.5, 0.1875, ((0, 32),)),
        "value_projection": scatter_about(key_list[4], (MODEL_WIDTH, KEY_VALUE_HEADS * HEAD_SIZE), MODEL_WIDTH ** -0.5, 0.1875, ((0, 32),)),
        "w_output": scatter_about(key_list[5], (MODEL_WIDTH, QUERY_HEADS * HEAD_SIZE), (max(1, QUERY_HEADS * HEAD_SIZE * 16 // SEQ_LEN)) ** -0.5, 2.0, ((0, 32),)),
        "w_zgate": scatter_about(key_list[6], (MODEL_WIDTH, DSSM), MODEL_WIDTH ** -0.5, 0.1875, ((0, 32),)),
        "w_inner": scatter_about(key_list[7], (MODEL_WIDTH, CONV), MODEL_WIDTH ** -0.5, 0.1875, ((0, 32),)),
        "w_step": scatter_about(key_list[8], (MODEL_WIDTH, H), MODEL_WIDTH ** -0.5, 0.1875, ((0, 32),)),
        "conv_taps": scatter_about(key_list[9], (KW, CONV), 0.5, 3.0, ((1, 32),)),
        "conv_bias": scatter_about(key_list[10], (CONV,), 0.5, 3.0, ((0, 32),)),
        "ssm_gain": jnp.clip(1.0 + 0.1 * jax.random.normal(key_list[11], (DSSM,), jnp.float32), 0.5, 1.5).astype(jnp.bfloat16),
        "w_mixout": scatter_about(key_list[12], (MODEL_WIDTH, DSSM), DSSM ** -0.5, 0.15625, ((0, 32),)),
        "gain_mlp": jnp.clip(1.0 + 0.1 * jax.random.normal(key_list[13], (MODEL_WIDTH,), jnp.float32), 0.5, 1.5).astype(jnp.bfloat16),
        "w_gate": scatter_about(key_list[14], (MODEL_WIDTH, FF), MODEL_WIDTH ** -0.5, 0.1875, ((0, 32),)),
        "w_up": scatter_about(key_list[15], (MODEL_WIDTH, FF), MODEL_WIDTH ** -0.5, 0.1875, ((0, 32),)),
        "w_down": scatter_about(key_list[16], (MODEL_WIDTH, FF), FF ** -0.5, 0.125, ((0, 32),)),
        "head_params": draw_head_params(jax.random.fold_in(key_list[19], 71), 0),
        "cotangent": noise_with(key_list[18], (TOKENS, MODEL_WIDTH), 1.0, 6.0, ((0, 32),), (0, 1, 32, 2.75)),
    }


epsilon = 1e-05
rope_base = 100000000000.0
highest = lax.Precision.HIGHEST

@jax.custom_vjp
def lowered_cast(v):
    return lax.optimization_barrier(v.astype(jnp.bfloat16)).astype(jnp.float32)

@jax.custom_vjp
def lowered_cast_pullback(v):
    return v

def low_keep(v):
    return (lowered_cast(v), None)

def low_pass(kept, grad):
    return (grad,)

def back_keep(v):
    return (v, None)

def back_low(kept, grad):
    return (lowered_cast(grad),)
lowered_cast.defvjp(low_keep, low_pass)
lowered_cast_pullback.defvjp(back_keep, back_low)

def matrix_multiply(left_rows, right_rows):
    return jnp.dot(left_rows, right_rows, precision=highest)

def rms_norm(rows_in, gain_vec):
    scale_rows = lax.rsqrt(lax.optimization_barrier(jnp.mean(rows_in * rows_in, axis=-1, keepdims=True)) + epsilon)
    return rows_in * scale_rows * gain_vec

def rotary_embedding(heads_in, token_positions):
    half_size = heads_in.shape[-1] // 2
    frequency = rope_base ** (-jnp.arange(half_size, dtype=jnp.float32) / half_size)
    angles = token_positions.astype(jnp.float32)[:, None] * frequency[None, :]
    cosine = jnp.cos(angles)[:, None, :]
    sine_table = jnp.sin(angles)[:, None, :]
    first_half = heads_in[..., :half_size]
    second_half = heads_in[..., half_size:]
    return jnp.concatenate([first_half * cosine - second_half * sine_table, second_half * cosine + first_half * sine_table], axis=-1)

def block_scan(state, block_in):
    x_in, b_in, c_in, step_in, log_in = block_in
    block_len = log_in.shape[0]
    cumulative = jnp.cumsum(log_in, axis=0)
    causal = (jnp.arange(block_len)[:, None] >= jnp.arange(block_len)[None, :]).astype(jnp.float32)
    cum_heads = cumulative.T
    exponent = jnp.where(causal[None] > 0, cum_heads[:, :, None] - cum_heads[:, None, :], 0.0)
    decay_mat = jnp.exp(exponent) * causal[None]
    inner_cb = jnp.dot(c_in, b_in.T, precision=highest)
    mixing = decay_mat * inner_cb[None] * step_in.T[:, None, :]
    intra = jnp.einsum('hts,shp->thp', mixing, x_in, precision=highest)
    inter = jnp.exp(cumulative)[:, :, None] * jnp.einsum('hpn,tn->thp', state, c_in, precision=highest)
    tail = jnp.exp(cumulative[-1][None, :] - cumulative) * step_in
    weighted = x_in * tail[:, :, None]
    new_state = jnp.exp(cumulative[-1])[:, None, None] * state + jnp.einsum('shp,sn->hpn', weighted, b_in, precision=highest)
    return (new_state, intra + inter)

def sequence_layer(tokens_seq, weights):
    gain_in, w_query, key_projection, value_projection, w_output, w_zgate, w_inner, w_step, conv_taps, conv_bias, ssm_gain, w_mixout, gain_mlp, w_gate, w_up, w_down, head_params = weights
    token_length = tokens_seq.shape[0]
    query_group_width = QUERY_HEADS // KEY_VALUE_HEADS
    token_positions = jnp.arange(token_length, dtype=jnp.int32)
    normalized_rows = lowered_cast(rms_norm(tokens_seq, gain_in))
    query_unrotated = lowered_cast_pullback(matrix_multiply(normalized_rows, w_query)).reshape(token_length, QUERY_HEADS, HEAD_SIZE)
    key_unrotated = lowered_cast_pullback(matrix_multiply(normalized_rows, key_projection)).reshape(token_length, KEY_VALUE_HEADS, HEAD_SIZE)
    value_token_rows = lowered_cast(lowered_cast_pullback(matrix_multiply(normalized_rows, value_projection))).reshape(token_length, KEY_VALUE_HEADS, HEAD_SIZE)
    query_rotated = lowered_cast(rotary_embedding(query_unrotated, token_positions)).reshape(token_length, KEY_VALUE_HEADS, query_group_width, HEAD_SIZE)
    key_rotated = lowered_cast(rotary_embedding(key_unrotated, token_positions))
    scores = lowered_cast_pullback(jnp.einsum('qgrd,kgd->grqk', query_rotated, key_rotated, precision=highest) * HEAD_SIZE ** (-0.5))
    causal = token_positions[:, None] >= token_positions[None, :]
    scores = jnp.where(causal[None, None], scores, -1e+30)
    probs = lowered_cast(jax.nn.softmax(scores, axis=-1))
    attended = jnp.einsum('grqk,kgd->qgrd', probs, value_token_rows, precision=highest).reshape(token_length, QUERY_HEADS * HEAD_SIZE)
    attended = lowered_cast(lowered_cast_pullback(attended))
    attn_rows = lowered_cast_pullback(matrix_multiply(attended, w_output.T))
    zgate_rows = lowered_cast_pullback(matrix_multiply(normalized_rows, w_zgate))
    inner_rows = lowered_cast_pullback(matrix_multiply(normalized_rows, w_inner))
    step_raw = lowered_cast_pullback(matrix_multiply(normalized_rows, w_step))
    padded = jnp.concatenate([jnp.zeros((KW - 1, CONV), jnp.float32), inner_rows], axis=0)
    conv_out = conv_bias[None, :] + padded[0:token_length] * conv_taps[0]
    for tap_index in range(1, KW):
        conv_out = conv_out + padded[tap_index:tap_index + token_length] * conv_taps[tap_index]
    activated = jax.nn.silu(conv_out)
    x_heads = activated[:, :DSSM].reshape(token_length, H, HEAD_SIZE)
    b_rows = activated[:, DSSM:DSSM + N]
    c_rows = activated[:, DSSM + N:]
    step_size = jax.nn.softplus(step_raw + head_params[0])
    log_decay = -step_size * jnp.exp(head_params[1])
    block_len = min(128, token_length)
    block_count = token_length // block_len
    blocks_in = (x_heads.reshape(block_count, block_len, H, HEAD_SIZE), b_rows.reshape(block_count, block_len, N), c_rows.reshape(block_count, block_len, N), step_size.reshape(block_count, block_len, H), log_decay.reshape(block_count, block_len, H))
    _, ssm_blocks = lax.scan(jax.checkpoint(block_scan), jnp.zeros((H, HEAD_SIZE, N), jnp.float32), blocks_in)
    ssm_out = ssm_blocks.reshape(token_length, H, HEAD_SIZE) + head_params[2][None, :, None] * x_heads
    gated = ssm_out.reshape(token_length, DSSM) * jax.nn.silu(zgate_rows)
    mixed_norm = lowered_cast(rms_norm(gated, ssm_gain))
    mix_rows = lowered_cast_pullback(matrix_multiply(mixed_norm, w_mixout.T))
    hidden = tokens_seq + attn_rows + mix_rows
    normed_mlp = lowered_cast(rms_norm(hidden, gain_mlp))
    gate_rows = lowered_cast_pullback(matrix_multiply(normed_mlp, w_gate))
    up_rows = lowered_cast_pullback(matrix_multiply(normed_mlp, w_up))
    act_rows = lowered_cast(jax.nn.silu(gate_rows) * up_rows)
    return hidden + matrix_multiply(act_rows, w_down.T)

def forward(tokens, gain_in, w_query, key_projection, value_projection, w_output, w_zgate, w_inner, w_step, conv_taps, conv_bias, ssm_gain, w_mixout, gain_mlp, w_gate, w_up, w_down, head_params):
    weights = (gain_in, w_query, key_projection, value_projection, w_output, w_zgate, w_inner, w_step, conv_taps, conv_bias, ssm_gain, w_mixout, gain_mlp, w_gate, w_up, w_down, head_params)
    sequences = tokens.reshape(TOKENS // SEQ_LEN, SEQ_LEN, MODEL_WIDTH)

    def one_sequence(carry, tokens_seq):
        return (carry, sequence_layer(tokens_seq, weights))
    _, outputs = lax.scan(jax.checkpoint(one_sequence), jnp.zeros((), jnp.float32), sequences)
    return outputs.reshape(TOKENS, MODEL_WIDTH)

def reference(tokens, gain_in, w_query, key_projection, value_projection, w_output, w_zgate, w_inner, w_step, conv_taps, conv_bias, ssm_gain, w_mixout, gain_mlp, w_gate, w_up, w_down, head_params, cotangent):
    inputs = [array_in.astype(jnp.float32) for array_in in (tokens, gain_in, w_query, key_projection, value_projection, w_output, w_zgate, w_inner, w_step, conv_taps, conv_bias, ssm_gain, w_mixout, gain_mlp, w_gate, w_up, w_down, head_params)]
    primal, pullback = jax.vjp(forward, *inputs)
    grads = pullback(cotangent.astype(jnp.float32))
    return (primal.astype(jnp.bfloat16), grads[0].astype(jnp.bfloat16), grads[1], grads[2], grads[3], grads[4], grads[5], grads[6], grads[7], grads[8], grads[9], grads[10], grads[11], grads[12], grads[13], grads[14], grads[15], grads[16], grads[17])
```

```python
import jax
import jax.numpy as jnp
from jax import lax
from jax.sharding import PartitionSpec as P

QUERY_HEADS = 8
KEY_VALUE_HEADS = 2
HEAD_SIZE = 64
H = 24
N = 128


epsilon = 1e-05
rope_base = 100000000000.0
highest = lax.Precision.HIGH
everywhere = ("dp", "seq")
chunk_rows = 128


def swapped(value, bit):
    count = lax.axis_size(everywhere)
    return lax.ppermute(value, everywhere, [(i, i ^ (1 << bit)) for i in range(count)])


def bit_order(turn):
    bits = lax.axis_size(everywhere).bit_length() - 1
    core = lax.axis_size("seq").bit_length() - 1
    others = [b for b in range(bits - 1, -1, -1) if b != core]
    heavy = others[::-1][turn % 3]
    return [b for b in others if b != heavy] + [heavy, core]


def gathered(block, turn):
    place = lax.axis_index(everywhere)
    value, have = block, []
    for bit in bit_order(turn):
        other = swapped(value, bit)
        axis = len([b for b in have if b > bit])
        value = jnp.where(
            (place >> bit) & 1 == 0,
            jnp.stack([value, other], axis),
            jnp.stack([other, value], axis),
        )
        have.append(bit)
    return value.reshape(-1, block.shape[1])


def reduced(total, turn):
    place, count = lax.axis_index(everywhere), lax.axis_size(everywhere)
    left = list(range(count.bit_length() - 2, -1, -1))
    value = total.reshape((2,) * len(left) + (total.shape[0] // count, total.shape[1]))
    for bit in bit_order(turn)[::-1]:
        axis = left.index(bit)
        mine = (place >> bit) & 1
        away = lax.dynamic_index_in_dim(value, 1 - mine, axis, False).astype(jnp.bfloat16)
        keep = lax.dynamic_index_in_dim(value, mine, axis, False)
        value = keep + swapped(away, bit).astype(jnp.float32)
        left.pop(axis)
    return value


def summed(value):
    for bit in bit_order(0):
        value = value + swapped(value, bit)
    return value


def passed_along(value, axis, steps):
    count = lax.axis_size(axis)
    initial, last = (max(0, -steps), min(count, count - steps))
    return lax.ppermute(value, axis, [(source, source + steps) for source in range(initial, last)])


def prefix(shard, axis, combine, identity):
    devices, index = (lax.axis_size(axis), lax.axis_index(axis))
    everything = jax.tree.map(
        lambda part, kind: lax.all_gather(part.astype(kind), axis),
        shard,
        (jnp.bfloat16, jnp.bfloat16),
    )
    start = jax.tree.map(
        lambda part, zero: jnp.broadcast_to(jnp.asarray(zero, part.dtype), part.shape),
        shard,
        identity,
    )

    def lap(k, before):
        reached = k < index
        new = combine(
            before, jax.tree.map(lambda part, own: part[k].astype(own.dtype), everything, shard)
        )
        return jax.tree.map(lambda a, b: jnp.where(reached, a, b), new, before)

    return lax.fori_loop(0, devices, lap, start)


def prefix_2(shard, axis, join, neutral):
    count = lax.axis_size(axis)
    place = lax.axis_index(axis)
    ahead = count - 1 - place
    gathered = jax.tree.map(
        lambda a, kind: lax.all_gather(a.astype(kind), axis),
        shard,
        jax.tree.map(lambda a: jnp.bfloat16 if a.dtype == jnp.float32 else a.dtype, shard),
    )
    state = jax.tree.map(lambda a, e: jnp.zeros_like(a) + jnp.asarray(e, a.dtype), shard, neutral)

    def one(lap, state):
        source = count - 1 - lap
        return join(
            state,
            jax.tree.map(
                lambda a, own: lax.dynamic_index_in_dim(a, source, 0, False).astype(own.dtype),
                gathered,
                shard,
            ),
        )

    return lax.fori_loop(0, ahead, one, state)


def rms_norm(rows_in, gain_vec):
    scale_rows = lax.rsqrt(jnp.mean(rows_in * rows_in, axis=-1, keepdims=True) + epsilon)
    return rows_in * scale_rows * gain_vec


def norm_back(rows_in, gain_vec, grad_rows):
    _, pullback = jax.vjp(rms_norm, rows_in, gain_vec)
    return pullback(grad_rows)


def rotary_tables(token_positions, half_size):
    frequency = rope_base ** (-jnp.arange(half_size, dtype=jnp.float32) / half_size)
    angles = token_positions.astype(jnp.float32)[:, None] * frequency[None, :]
    return (jnp.cos(angles)[:, None, :], jnp.sin(angles)[:, None, :])


def rotary_embedding(heads_in, token_positions):
    half_size = heads_in.shape[-1] // 2
    cosine, sine_table = rotary_tables(token_positions, half_size)
    first_half = heads_in[..., :half_size]
    second_half = heads_in[..., half_size:]
    return jnp.concatenate(
        [
            first_half * cosine - second_half * sine_table,
            second_half * cosine + first_half * sine_table,
        ],
        axis=-1,
    )


def rotary_embedding_pullback(grad_heads, token_positions):
    half_size = grad_heads.shape[-1] // 2
    cosine, sine_table = rotary_tables(token_positions, half_size)
    first_half = grad_heads[..., :half_size]
    second_half = grad_heads[..., half_size:]
    return jnp.concatenate(
        [
            first_half * cosine + second_half * sine_table,
            second_half * cosine - first_half * sine_table,
        ],
        axis=-1,
    )


def matrix_product(left_rows, right_rows):
    return jnp.dot(left_rows, right_rows, preferred_element_type=jnp.float32)


def product_back(left_rows, right_rows):
    return jnp.einsum("tf,df->td", left_rows, right_rows, preferred_element_type=jnp.float32)


def product_outer(left_rows, right_rows):
    return jnp.einsum("td,tf->df", left_rows, right_rows, preferred_element_type=jnp.float32)


def swiglu(gate_in, up_in):
    return jax.nn.silu(gate_in) * up_in


def conv_piece(padded, step_raw, conv_taps, conv_bias, head_params):
    width = conv_taps.shape[0]
    token_length = padded.shape[0] - width + 1
    conv_out = conv_bias[None, :] + padded[0:token_length] * conv_taps[0]
    for tap_index in range(1, width):
        conv_out = conv_out + padded[tap_index : tap_index + token_length] * conv_taps[tap_index]
    activated = jax.nn.silu(conv_out)
    ssm_width = H * HEAD_SIZE
    x_heads = activated[:, :ssm_width].reshape(token_length, H, HEAD_SIZE)
    b_rows = activated[:, ssm_width : ssm_width + N]
    c_rows = activated[:, ssm_width + N :]
    step_size = jax.nn.softplus(step_raw + head_params[0])
    cumulative = jnp.cumsum(-step_size * jnp.exp(head_params[1]), axis=0)
    return (x_heads, b_rows, c_rows, step_size, cumulative)


def state_piece(x_heads, b_rows, step_size, cumulative):
    tail = jnp.exp(cumulative[-1][None, :] - cumulative) * step_size
    weighted = x_heads * tail[:, :, None]
    local_state = jnp.einsum("shp,sn->hpn", weighted, b_rows, precision=highest)
    return (local_state, jnp.exp(cumulative[-1]))


def output_piece(
    x_heads, b_rows, c_rows, step_size, cumulative, state_in, zgate_rows, ssm_gain, head_params
):
    token_length = x_heads.shape[0]
    length = min(chunk_rows, token_length)
    chunks = token_length // length
    causal = jnp.arange(length)[:, None] >= jnp.arange(length)[None, :]
    in_chunks = cumulative.reshape(chunks, length, H)
    ends = in_chunks[:, -1]
    starts = jnp.concatenate([jnp.zeros_like(ends[:1]), ends[:-1]], axis=0)
    relative = in_chunks - starts[:, None]
    x_chunks = x_heads.reshape(chunks, length, H, HEAD_SIZE)
    b_chunks = b_rows.reshape(chunks, length, N)
    c_chunks = c_rows.reshape(chunks, length, N)
    steps = step_size.reshape(chunks, length, H)
    by_head = relative.transpose(0, 2, 1)
    exponent = jnp.where(causal, by_head[:, :, :, None] - by_head[:, :, None, :], 0.0)
    decay_mat = jnp.where(causal, jnp.exp(exponent), 0.0)
    inner_cb = jnp.einsum("ctn,csn->cts", c_chunks, b_chunks, precision=highest)
    mixing = decay_mat * inner_cb[:, None] * steps.transpose(0, 2, 1)[:, :, None, :]
    intra = jnp.einsum("chts,cshp->cthp", mixing, x_chunks, precision=highest)
    whole = ends - starts
    tail = jnp.exp(whole[:, None] - relative) * steps
    local = jnp.einsum("cshp,csn->chpn", x_chunks * tail[..., None], b_chunks, precision=highest)
    decays = jnp.exp(whole)
    states = [state_in]
    for chunk in range(chunks - 1):
        states.append(decays[chunk][:, None, None] * states[-1] + local[chunk])
    inter = jnp.exp(relative)[..., None] * jnp.einsum(
        "chpn,ctn->cthp", jnp.stack(states), c_chunks, precision=highest
    )
    ssm_out = (intra + inter).reshape(x_heads.shape) + head_params[2][None, :, None] * x_heads
    gated = ssm_out.reshape(token_length, H * HEAD_SIZE) * jax.nn.silu(zgate_rows)
    return rms_norm(gated, ssm_gain)


def chain_combine(earlier, later):
    return (earlier[0] * later[0], later[0][:, None, None] * earlier[1] + later[1])


def back_combine(earlier, later):
    return (later[0] * earlier[0], later[1] + later[0][:, None, None] * earlier[1])


def attention_scores(query_grouped, key_grouped, token_positions, total_length):
    scores = jnp.einsum(
        "qgrd,kgd->grqk", query_grouped, key_grouped, preferred_element_type=jnp.float32
    ) * HEAD_SIZE ** (-0.5)
    causal = token_positions[:, None] >= jnp.arange(total_length, dtype=jnp.int32)[None, :]
    return jnp.where(causal[None, None], scores, -1e30)


def shards(
    tokens,
    gain_in,
    w_query,
    key_projection,
    value_projection,
    w_output,
    w_zgate,
    w_inner,
    w_step,
    conv_taps,
    conv_bias,
    ssm_gain,
    w_mixout,
    gain_mlp,
    w_gate,
    w_up,
    w_down,
    head_params,
    cotangent,
):
    shard_rows = w_query.shape[0]
    count = lax.axis_size(everywhere)
    heads_width, pair_width = QUERY_HEADS * HEAD_SIZE, KEY_VALUE_HEADS * HEAD_SIZE
    vectors = (conv_taps, conv_bias, ssm_gain, gain_in, gain_mlp)
    extents = [vector.size for vector in vectors]
    edges = [sum(extents[:i]) for i in range(len(extents) + 1)]
    extra = -(-edges[-1] // shard_rows)
    spare = extra * shard_rows - edges[-1]
    margin = -(extra + H) % 128
    flat = jnp.concatenate([v.reshape(-1) for v in vectors] + [jnp.zeros((spare,), jnp.bfloat16)])
    small = jnp.concatenate(
        [w_step, flat.reshape(shard_rows, extra), jnp.zeros((shard_rows, margin), jnp.bfloat16)],
        axis=1,
    )
    inner_w = gathered(jnp.concatenate([w_inner, small], axis=1), 0)
    head_w = gathered(jnp.concatenate([w_query, key_projection, value_projection], axis=1), 2)
    zgate_w = gathered(w_zgate, 1)
    held_back = lax.optimization_barrier(
        (inner_w, head_w, zgate_w, w_output, w_mixout, w_gate, w_up, w_down)
    )
    inner_w, head_w, zgate_w, w_output, w_mixout, w_gate, w_up, w_down = held_back
    branch_w = gathered(jnp.concatenate([w_output, w_mixout], axis=1), 0)
    gate_w = gathered(w_gate, 1)
    up_w = gathered(w_up, 2)
    down_w = gathered(w_down, 0)
    small_w = inner_w[:, w_inner.shape[1] :]
    inner_w = inner_w[:, : w_inner.shape[1]]
    query_w = head_w[:, :heads_width]
    key_weight_full = head_w[:, heads_width : heads_width + pair_width]
    value_w = head_w[:, heads_width + pair_width :]
    output_w = branch_w[:, : w_output.shape[1]]
    mixout_w = branch_w[:, w_output.shape[1] :]
    step_w = small_w[:, :H]
    packed = small_w[:, H : H + extra].reshape(count, shard_rows * extra)
    pieces = [packed[:, edges[i] : edges[i + 1]] for i in range(len(vectors))]
    taps_full = (
        pieces[0].reshape(count, *conv_taps.shape).transpose(1, 0, 2).reshape(len(conv_taps), -1)
    )
    cbias_full, ssm_gain_f, gain_in_f, gain_mlp_f = [piece.reshape(-1) for piece in pieces[1:]]
    token_length = tokens.shape[0]
    total_length = token_length * lax.axis_size("seq")
    query_group_width = QUERY_HEADS // KEY_VALUE_HEADS
    width = conv_taps.shape[0]
    token_positions = lax.axis_index("seq") * token_length + jnp.arange(
        token_length, dtype=jnp.int32
    )
    tokens_f = tokens.astype(jnp.float32)
    normalized_rows = rms_norm(tokens_f, gain_in_f.astype(jnp.float32)).astype(jnp.bfloat16)
    query_rotated = rotary_embedding(
        matrix_product(normalized_rows, query_w).reshape(token_length, QUERY_HEADS, HEAD_SIZE),
        token_positions,
    ).astype(jnp.bfloat16)
    key_rotated = rotary_embedding(
        matrix_product(normalized_rows, key_weight_full).reshape(
            token_length, KEY_VALUE_HEADS, HEAD_SIZE
        ),
        token_positions,
    ).astype(jnp.bfloat16)
    value_low = matrix_product(normalized_rows, value_w).astype(jnp.bfloat16)
    key_full_rows, value_full_rows = (
        lax.all_gather(
            key_rotated.reshape(token_length, KEY_VALUE_HEADS * HEAD_SIZE),
            "seq",
            axis=0,
            tiled=True,
        ),
        lax.all_gather(value_low, "seq", axis=0, tiled=True),
    )
    query_grouped = query_rotated.reshape(
        token_length, KEY_VALUE_HEADS, query_group_width, HEAD_SIZE
    )
    key_grouped = key_full_rows.reshape(total_length, KEY_VALUE_HEADS, HEAD_SIZE)
    value_grouped = value_full_rows.reshape(total_length, KEY_VALUE_HEADS, HEAD_SIZE)
    scores = attention_scores(query_grouped, key_grouped, token_positions, total_length)
    row_max = jnp.max(scores, axis=-1, keepdims=True)
    expo_rows = jnp.exp(scores - row_max)
    row_total = jnp.sum(expo_rows, axis=-1, keepdims=True)
    log_total = row_max + jnp.log(row_total)
    soft_low = (expo_rows / row_total).astype(jnp.bfloat16)
    attended = (
        jnp.einsum("grqk,kgd->qgrd", soft_low, value_grouped, preferred_element_type=jnp.float32)
        .reshape(token_length, QUERY_HEADS * HEAD_SIZE)
        .astype(jnp.bfloat16)
    )
    attn_rows = product_back(attended, output_w)
    zgate_rows = matrix_product(normalized_rows, zgate_w)
    inner_rows = matrix_product(normalized_rows, inner_w)
    step_raw = matrix_product(normalized_rows, step_w)
    rim_rows = passed_along(inner_rows[token_length - (width - 1) :], "seq", 1)
    padded = jnp.concatenate([rim_rows, inner_rows], axis=0)
    x_heads, b_rows, c_rows, step_size, cumulative = conv_piece(
        padded, step_raw, taps_full.astype(jnp.float32), cbias_full.astype(jnp.float32), head_params
    )
    local_state, total_decay = state_piece(x_heads, b_rows, step_size, cumulative)
    decay_in, state_in = prefix(
        (total_decay, local_state),
        "seq",
        chain_combine,
        (jnp.ones_like(total_decay), jnp.zeros_like(local_state)),
    )
    mixed_norm = output_piece(
        x_heads,
        b_rows,
        c_rows,
        step_size,
        cumulative,
        state_in,
        zgate_rows,
        ssm_gain_f.astype(jnp.float32),
        head_params,
    )
    mixed_low = mixed_norm.astype(jnp.bfloat16)
    mix_rows = product_back(mixed_low, mixout_w)
    hidden = tokens_f + attn_rows + mix_rows
    normed_mlp = rms_norm(hidden, gain_mlp_f.astype(jnp.float32)).astype(jnp.bfloat16)
    gate_rows = matrix_product(normed_mlp, gate_w)
    up_rows = matrix_product(normed_mlp, up_w)
    act_rows = swiglu(gate_rows, up_rows).astype(jnp.bfloat16)
    output = (hidden + product_back(act_rows, down_w)).astype(jnp.bfloat16)
    grad_act = matrix_product(cotangent, down_w)
    grad_wdown = product_outer(cotangent, act_rows)
    _, swiglu_pull = jax.vjp(swiglu, gate_rows, up_rows)
    grad_gate_f, grad_up_f = swiglu_pull(grad_act)
    grad_gate = grad_gate_f.astype(jnp.bfloat16)
    grad_up = grad_up_f.astype(jnp.bfloat16)
    grad_normed_mlp = product_back(grad_gate, gate_w) + product_back(grad_up, up_w)
    grad_wgate = product_outer(normed_mlp, grad_gate)
    grad_wup = product_outer(normed_mlp, grad_up)
    grad_hidden_norm, grad_gain_mlp_rows = norm_back(
        hidden, gain_mlp_f.astype(jnp.float32), grad_normed_mlp
    )
    grad_hidden = cotangent.astype(jnp.float32) + grad_hidden_norm
    shard_wdown = reduced(grad_wdown, 0)
    shard_wgate = reduced(grad_wgate, 1)
    shard_wup = reduced(grad_wup, 2)
    branch_gradient = grad_hidden.astype(jnp.bfloat16)
    grad_wout = product_outer(branch_gradient, attended)
    grad_wmixout = product_outer(branch_gradient, mixed_low)
    shard_branch = reduced(jnp.concatenate([grad_wout, grad_wmixout], axis=1), 0)
    grad_mixed = matrix_product(branch_gradient, mixout_w)
    grad_attended = (
        matrix_product(branch_gradient, output_w)
        .astype(jnp.bfloat16)
        .reshape(token_length, KEY_VALUE_HEADS, query_group_width, HEAD_SIZE)
    )
    scores_again = attention_scores(query_grouped, key_grouped, token_positions, total_length)
    soft_rows = jnp.exp(scores_again - log_total)
    soft_again = soft_rows.astype(jnp.bfloat16)
    grad_soft = jnp.einsum(
        "qgrd,kgd->grqk", grad_attended, value_grouped, preferred_element_type=jnp.float32
    )
    gradient_value_full = jnp.einsum(
        "grqk,qgrd->kgd", soft_again, grad_attended, preferred_element_type=jnp.float32
    )
    row_delta = jnp.sum(soft_rows * grad_soft, axis=-1, keepdims=True)
    grad_scores = (soft_rows * (grad_soft - row_delta)).astype(jnp.bfloat16)
    grad_query_rot = jnp.einsum(
        "grqk,kgd->qgrd", grad_scores, key_grouped, preferred_element_type=jnp.float32
    ) * HEAD_SIZE ** (-0.5)
    gradient_key_full = jnp.einsum(
        "grqk,qgrd->kgd", grad_scores, query_grouped, preferred_element_type=jnp.float32
    ) * HEAD_SIZE ** (-0.5)
    gradient_key_rotated, grad_value_f = (
        lax.psum_scatter(
            gradient_key_full.reshape(total_length, KEY_VALUE_HEADS * HEAD_SIZE).astype(
                jnp.bfloat16
            ),
            "seq",
            scatter_dimension=0,
            tiled=True,
        ).astype(jnp.float32),
        lax.psum_scatter(
            gradient_value_full.reshape(total_length, KEY_VALUE_HEADS * HEAD_SIZE).astype(
                jnp.bfloat16
            ),
            "seq",
            scatter_dimension=0,
            tiled=True,
        ).astype(jnp.float32),
    )
    grad_query = (
        rotary_embedding_pullback(
            grad_query_rot.reshape(token_length, QUERY_HEADS, HEAD_SIZE), token_positions
        )
        .reshape(token_length, QUERY_HEADS * HEAD_SIZE)
        .astype(jnp.bfloat16)
    )
    grad_key = (
        rotary_embedding_pullback(
            gradient_key_rotated.reshape(token_length, KEY_VALUE_HEADS, HEAD_SIZE), token_positions
        )
        .reshape(token_length, KEY_VALUE_HEADS * HEAD_SIZE)
        .astype(jnp.bfloat16)
    )
    grad_value = grad_value_f.astype(jnp.bfloat16)
    _, output_pull = jax.vjp(
        output_piece,
        x_heads,
        b_rows,
        c_rows,
        step_size,
        cumulative,
        state_in,
        zgate_rows,
        ssm_gain_f.astype(jnp.float32),
        head_params,
    )
    out_x, out_b, out_c, out_step, out_cum, out_state, out_zgate, grad_ssm_gain_rows, out_head = (
        output_pull(grad_mixed)
    )
    decay_after, state_grad = prefix_2(
        (total_decay, out_state),
        "seq",
        back_combine,
        (jnp.ones_like(total_decay), jnp.zeros_like(out_state)),
    )
    grad_decay = jnp.sum(state_grad * state_in, axis=(1, 2))
    _, state_pull = jax.vjp(state_piece, x_heads, b_rows, step_size, cumulative)
    state_x, state_b, state_step, state_cum = state_pull((state_grad, grad_decay))
    _, conv_pull = jax.vjp(
        conv_piece,
        padded,
        step_raw,
        taps_full.astype(jnp.float32),
        cbias_full.astype(jnp.float32),
        head_params,
    )
    grad_padded, grad_step_raw, grad_taps, grad_cbias, conv_head = conv_pull(
        (out_x + state_x, out_b + state_b, out_c, out_step + state_step, out_cum + state_cum)
    )
    rim_back = passed_along(grad_padded[: width - 1], "seq", -1)
    grad_inner = grad_padded[width - 1 :] + jnp.concatenate(
        [jnp.zeros((token_length - (width - 1), grad_padded.shape[1]), jnp.float32), rim_back],
        axis=0,
    )
    grad_inner_low = grad_inner.astype(jnp.bfloat16)
    grad_zgate_low = out_zgate.astype(jnp.bfloat16)
    grad_step_low = grad_step_raw.astype(jnp.bfloat16)
    grad_normed = (
        product_back(grad_query, query_w)
        + product_back(grad_key, key_weight_full)
        + product_back(grad_value, value_w)
        + product_back(grad_zgate_low, zgate_w)
        + product_back(grad_inner_low, inner_w)
        + product_back(grad_step_low, step_w)
    )
    shard_heads = reduced(
        product_outer(
            normalized_rows, jnp.concatenate([grad_query, grad_key, grad_value], axis=1)
        ),
        0,
    )
    shard_wzgate = reduced(product_outer(normalized_rows, grad_zgate_low), 1)
    shard_winner = reduced(product_outer(normalized_rows, grad_inner_low), 2)
    grad_wstep = product_outer(normalized_rows, grad_step_low)
    grad_tokens_norm, grad_gain_in_rows = norm_back(
        tokens_f, gain_in_f.astype(jnp.float32), grad_normed
    )
    grad_tokens = (grad_hidden + grad_tokens_norm).astype(jnp.bfloat16)
    taps_by_owner = grad_taps.reshape(len(conv_taps), count, -1).transpose(1, 0, 2)
    by_owner = [taps_by_owner.reshape(count, -1)] + [
        vector.reshape(count, -1)
        for vector in (grad_cbias, grad_ssm_gain_rows, grad_gain_in_rows, grad_gain_mlp_rows)
    ]
    by_owner.append(jnp.zeros((count, spare), jnp.float32))
    shard_small = reduced(
        jnp.concatenate(
            [
                grad_wstep,
                jnp.concatenate(by_owner, axis=1).reshape(count * shard_rows, extra),
                jnp.zeros((count * shard_rows, margin), jnp.float32),
            ],
            axis=1,
        ),
        0,
    )
    shard_flat = shard_small[:, H : H + extra].reshape(-1)
    shard_vectors = [
        shard_flat[edges[i] : edges[i + 1]].reshape(vectors[i].shape) for i in range(len(vectors))
    ]
    grad_head = summed(out_head + conv_head)
    return (
        output,
        grad_tokens,
        shard_vectors[3],
        shard_heads[:, :heads_width],
        shard_heads[:, heads_width : heads_width + pair_width],
        shard_heads[:, heads_width + pair_width :],
        shard_branch[:, : w_output.shape[1]],
        shard_wzgate,
        shard_winner,
        shard_small[:, :H],
        shard_vectors[0],
        shard_vectors[1],
        shard_vectors[2],
        shard_branch[:, w_output.shape[1] :],
        shard_vectors[4],
        shard_wgate,
        shard_wup,
        shard_wdown,
        grad_head,
    )


def solution(mesh):
    return jax.shard_map(
        shards,
        mesh=mesh,
        in_specs=(
            P(("dp", "seq"), None),
            P(("dp", "seq")),
            P(("dp", "seq"), None),
            P(("dp", "seq"), None),
            P(("dp", "seq"), None),
            P(("dp", "seq"), None),
            P(("dp", "seq"), None),
            P(("dp", "seq"), None),
            P(("dp", "seq"), None),
            P(None, ("dp", "seq")),
            P(("dp", "seq")),
            P(("dp", "seq")),
            P(("dp", "seq"), None),
            P(("dp", "seq")),
            P(("dp", "seq"), None),
            P(("dp", "seq"), None),
            P(("dp", "seq"), None),
            P(),
            P(("dp", "seq"), None),
        ),
        out_specs=(
            P(("dp", "seq"), None),
            P(("dp", "seq"), None),
            P(("dp", "seq")),
            P(("dp", "seq"), None),
            P(("dp", "seq"), None),
            P(("dp", "seq"), None),
            P(("dp", "seq"), None),
            P(("dp", "seq"), None),
            P(("dp", "seq"), None),
            P(("dp", "seq"), None),
            P(None, ("dp", "seq")),
            P(("dp", "seq")),
            P(("dp", "seq")),
            P(("dp", "seq"), None),
            P(("dp", "seq")),
            P(("dp", "seq"), None),
            P(("dp", "seq"), None),
            P(("dp", "seq"), None),
            P(),
        ),
        check_vma=False,
    )
```

```python
import jax
import jax.numpy as jnp
from jax import lax
from jax.sharding import PartitionSpec as P

QUERY_HEADS = 8
KEY_VALUE_HEADS = 2
HEAD_SIZE = 64
H = 24
N = 128


epsilon = 1e-05
rope_base = 100000000000.0
highest = lax.Precision.HIGH
everywhere = ("dp", "seq")
chunk_rows = 128


def swapped(value, bit):
    count = lax.axis_size(everywhere)
    return lax.ppermute(value, everywhere, [(i, i ^ (1 << bit)) for i in range(count)])


def bit_order(turn):
    bits = lax.axis_size(everywhere).bit_length() - 1
    core = lax.axis_size("seq").bit_length() - 1
    others = [b for b in range(bits - 1, -1, -1) if b != core]
    heavy = others[::-1][turn % 3]
    return [b for b in others if b != heavy] + [heavy, core]


def widened(value, order, step):
    bit, have = order[step], order[:step]
    other = swapped(value, bit)
    axis = len([b for b in have if b > bit])
    return jnp.where(
        (lax.axis_index(everywhere) >> bit) & 1 == 0,
        jnp.stack([value, other], axis),
        jnp.stack([other, value], axis),
    )


def gathered(block, order):
    value = block
    for step in range(len(order)):
        value = widened(value, order, step)
    return value.reshape(-1, block.shape[1])


def along_seq(block):
    order = list(range(lax.axis_size("seq").bit_length() - 1))
    parts = gathered(block.reshape(-1, block.shape[-1]), order)
    return parts.reshape((-1,) + block.shape)


def opened(total):
    count = lax.axis_size(everywhere)
    return total.reshape(
        (2,) * (count.bit_length() - 1) + (total.shape[0] // count, total.shape[1])
    )


def narrowed(value, turn, step):
    order = bit_order(turn)[::-1]
    bit = order[step]
    axis = len([b for b in order[step:] if b > bit])
    mine = (lax.axis_index(everywhere) >> bit) & 1
    away = lax.dynamic_index_in_dim(value, 1 - mine, axis, False).astype(jnp.bfloat16)
    keep = lax.dynamic_index_in_dim(value, mine, axis, False)
    return keep + swapped(away, bit).astype(jnp.float32)


def narrowed_all(values, turns, first, last):
    for step in range(first, last):
        values = [narrowed(value, turn, step) for value, turn in zip(values, turns)]
    return values


def reduced(total, turn):
    steps = len(bit_order(turn))
    return narrowed_all([opened(total)], [turn], 0, steps)[0]


def together(values, *others):
    return lax.optimization_barrier((values, others))


def summed(value):
    for bit in bit_order(0):
        value = value + swapped(value, bit)
    return value


def passed_along(value, axis, steps):
    count = lax.axis_size(axis)
    initial, last = (max(0, -steps), min(count, count - steps))
    return lax.ppermute(value, axis, [(source, source + steps) for source in range(initial, last)])


def prefix(shard, axis, combine, identity):
    devices, index = (lax.axis_size(axis), lax.axis_index(axis))
    everything = jax.tree.map(
        lambda part, kind: along_seq(part.astype(kind)),
        shard,
        (jnp.bfloat16, jnp.bfloat16),
    )
    start = jax.tree.map(
        lambda part, zero: jnp.broadcast_to(jnp.asarray(zero, part.dtype), part.shape),
        shard,
        identity,
    )

    def lap(k, before):
        reached = k < index
        new = combine(
            before, jax.tree.map(lambda part, own: part[k].astype(own.dtype), everything, shard)
        )
        return jax.tree.map(lambda a, b: jnp.where(reached, a, b), new, before)

    return lax.fori_loop(0, devices, lap, start)


def prefix_2(shard, axis, join, neutral):
    count = lax.axis_size(axis)
    place = lax.axis_index(axis)
    ahead = count - 1 - place
    gathered = jax.tree.map(
        lambda a, kind: along_seq(a.astype(kind)),
        shard,
        jax.tree.map(lambda a: jnp.bfloat16 if a.dtype == jnp.float32 else a.dtype, shard),
    )
    state = jax.tree.map(lambda a, e: jnp.zeros_like(a) + jnp.asarray(e, a.dtype), shard, neutral)

    def one(lap, state):
        source = count - 1 - lap
        return join(
            state,
            jax.tree.map(
                lambda a, own: lax.dynamic_index_in_dim(a, source, 0, False).astype(own.dtype),
                gathered,
                shard,
            ),
        )

    return lax.fori_loop(0, ahead, one, state)


def rms_norm(rows_in, gain_vec):
    scale_rows = lax.rsqrt(jnp.mean(rows_in * rows_in, axis=-1, keepdims=True) + epsilon)
    return rows_in * scale_rows * gain_vec


def norm_back(rows_in, gain_vec, grad_rows):
    _, pullback = jax.vjp(rms_norm, rows_in, gain_vec)
    return pullback(grad_rows)


def rotary_tables(token_positions, half_size):
    frequency = rope_base ** (-jnp.arange(half_size, dtype=jnp.float32) / half_size)
    angles = token_positions.astype(jnp.float32)[:, None] * frequency[None, :]
    return (jnp.cos(angles)[:, None, :], jnp.sin(angles)[:, None, :])


def rotary_embedding(heads_in, token_positions):
    half_size = heads_in.shape[-1] // 2
    cosine, sine_table = rotary_tables(token_positions, half_size)
    first_half = heads_in[..., :half_size]
    second_half = heads_in[..., half_size:]
    return jnp.concatenate(
        [
            first_half * cosine - second_half * sine_table,
            second_half * cosine + first_half * sine_table,
        ],
        axis=-1,
    )


def rotary_embedding_pullback(grad_heads, token_positions):
    half_size = grad_heads.shape[-1] // 2
    cosine, sine_table = rotary_tables(token_positions, half_size)
    first_half = grad_heads[..., :half_size]
    second_half = grad_heads[..., half_size:]
    return jnp.concatenate(
        [
            first_half * cosine + second_half * sine_table,
            second_half * cosine - first_half * sine_table,
        ],
        axis=-1,
    )


def matrix_product(left_rows, right_rows):
    return jnp.dot(left_rows, right_rows, preferred_element_type=jnp.float32)


def product_back(left_rows, right_rows):
    return jnp.einsum("tf,df->td", left_rows, right_rows, preferred_element_type=jnp.float32)


def product_outer(left_rows, right_rows):
    return jnp.einsum("td,tf->df", left_rows, right_rows, preferred_element_type=jnp.float32)


def swiglu(gate_in, up_in):
    return jax.nn.silu(gate_in) * up_in


def conv_piece(padded, step_raw, conv_taps, conv_bias, head_params):
    width = conv_taps.shape[0]
    token_length = padded.shape[0] - width + 1
    conv_out = conv_bias[None, :] + padded[0:token_length] * conv_taps[0]
    for tap_index in range(1, width):
        conv_out = conv_out + padded[tap_index : tap_index + token_length] * conv_taps[tap_index]
    activated = jax.nn.silu(conv_out)
    ssm_width = H * HEAD_SIZE
    x_heads = activated[:, :ssm_width].reshape(token_length, H, HEAD_SIZE)
    b_rows = activated[:, ssm_width : ssm_width + N]
    c_rows = activated[:, ssm_width + N :]
    step_size = jax.nn.softplus(step_raw + head_params[0])
    cumulative = jnp.cumsum(-step_size * jnp.exp(head_params[1]), axis=0)
    return (x_heads, b_rows, c_rows, step_size, cumulative)


def state_piece(x_heads, b_rows, step_size, cumulative):
    tail = jnp.exp(cumulative[-1][None, :] - cumulative) * step_size
    weighted = x_heads * tail[:, :, None]
    local_state = jnp.einsum("shp,sn->hpn", weighted, b_rows, precision=highest)
    return (local_state, jnp.exp(cumulative[-1]))


def output_piece(
    x_heads, b_rows, c_rows, step_size, cumulative, state_in, zgate_rows, ssm_gain, head_params
):
    token_length = x_heads.shape[0]
    length = min(chunk_rows, token_length)
    chunks = token_length // length
    causal = jnp.arange(length)[:, None] >= jnp.arange(length)[None, :]
    in_chunks = cumulative.reshape(chunks, length, H)
    ends = in_chunks[:, -1]
    starts = jnp.concatenate([jnp.zeros_like(ends[:1]), ends[:-1]], axis=0)
    relative = in_chunks - starts[:, None]
    x_chunks = x_heads.reshape(chunks, length, H, HEAD_SIZE)
    b_chunks = b_rows.reshape(chunks, length, N)
    c_chunks = c_rows.reshape(chunks, length, N)
    steps = step_size.reshape(chunks, length, H)
    by_head = relative.transpose(0, 2, 1)
    exponent = jnp.where(causal, by_head[:, :, :, None] - by_head[:, :, None, :], 0.0)
    decay_mat = jnp.where(causal, jnp.exp(exponent), 0.0)
    inner_cb = jnp.einsum("ctn,csn->cts", c_chunks, b_chunks, precision=highest)
    mixing = decay_mat * inner_cb[:, None] * steps.transpose(0, 2, 1)[:, :, None, :]
    intra = jnp.einsum("chts,cshp->cthp", mixing, x_chunks, precision=highest)
    whole = ends - starts
    tail = jnp.exp(whole[:, None] - relative) * steps
    local = jnp.einsum("cshp,csn->chpn", x_chunks * tail[..., None], b_chunks, precision=highest)
    decays = jnp.exp(whole)
    states = [state_in]
    for chunk in range(chunks - 1):
        states.append(decays[chunk][:, None, None] * states[-1] + local[chunk])
    inter = jnp.exp(relative)[..., None] * jnp.einsum(
        "chpn,ctn->cthp", jnp.stack(states), c_chunks, precision=highest
    )
    ssm_out = (intra + inter).reshape(x_heads.shape) + head_params[2][None, :, None] * x_heads
    gated = ssm_out.reshape(token_length, H * HEAD_SIZE) * jax.nn.silu(zgate_rows)
    return rms_norm(gated, ssm_gain)


def chain_combine(earlier, later):
    return (earlier[0] * later[0], later[0][:, None, None] * earlier[1] + later[1])


def back_combine(earlier, later):
    return (later[0] * earlier[0], later[1] + later[0][:, None, None] * earlier[1])


def attention_scores(query_grouped, key_grouped, token_positions, total_length):
    scores = jnp.einsum(
        "qgrd,kgd->grqk", query_grouped, key_grouped, preferred_element_type=jnp.float32
    ) * HEAD_SIZE ** (-0.5)
    causal = token_positions[:, None] >= jnp.arange(total_length, dtype=jnp.int32)[None, :]
    return jnp.where(causal[None, None], scores, -1e30)


def shards(
    tokens,
    gain_in,
    w_query,
    key_projection,
    value_projection,
    w_output,
    w_zgate,
    w_inner,
    w_step,
    conv_taps,
    conv_bias,
    ssm_gain,
    w_mixout,
    gain_mlp,
    w_gate,
    w_up,
    w_down,
    head_params,
    cotangent,
):
    shard_rows = w_query.shape[0]
    count = lax.axis_size(everywhere)
    heads_width, pair_width = QUERY_HEADS * HEAD_SIZE, KEY_VALUE_HEADS * HEAD_SIZE
    vectors = (conv_taps, conv_bias, ssm_gain, gain_in, gain_mlp)
    extents = [vector.size for vector in vectors]
    edges = [sum(extents[:i]) for i in range(len(extents) + 1)]
    extra = -(-edges[-1] // shard_rows)
    spare = extra * shard_rows - edges[-1]
    margin = -(extra + H) % 128
    flat = jnp.concatenate([v.reshape(-1) for v in vectors] + [jnp.zeros((spare,), jnp.bfloat16)])
    small = jnp.concatenate(
        [w_step, flat.reshape(shard_rows, extra), jnp.zeros((shard_rows, margin), jnp.bfloat16)],
        axis=1,
    )
    inner_w = gathered(jnp.concatenate([w_inner, small], axis=1), bit_order(0))
    head_w = gathered(
        jnp.concatenate([w_query, key_projection, value_projection], axis=1), bit_order(2)
    )
    zgate_w = gathered(w_zgate, bit_order(1))
    held_back = lax.optimization_barrier(
        (inner_w, head_w, zgate_w, w_output, w_mixout, w_gate, w_up, w_down)
    )
    inner_w, head_w, zgate_w, w_output, w_mixout, w_gate, w_up, w_down = held_back
    steps = count.bit_length() - 1
    turns = (0, 1, 2, 0)

    def further(blocks, first, last):
        for step in range(first, last):
            blocks = [
                widened(block, bit_order(turn), step) for block, turn in zip(blocks, turns)
            ]
        return blocks

    far = [jnp.concatenate([w_output, w_mixout], axis=1), w_gate, w_up, w_down]
    far = further(far, 0, steps - 3)
    small_w = inner_w[:, w_inner.shape[1] :]
    inner_w = inner_w[:, : w_inner.shape[1]]
    query_w = head_w[:, :heads_width]
    key_weight_full = head_w[:, heads_width : heads_width + pair_width]
    value_w = head_w[:, heads_width + pair_width :]
    step_w = small_w[:, :H]
    packed = small_w[:, H : H + extra].reshape(count, shard_rows * extra)
    pieces = [packed[:, edges[i] : edges[i + 1]] for i in range(len(vectors))]
    taps_full = (
        pieces[0].reshape(count, *conv_taps.shape).transpose(1, 0, 2).reshape(len(conv_taps), -1)
    )
    cbias_full, ssm_gain_f, gain_in_f, gain_mlp_f = [piece.reshape(-1) for piece in pieces[1:]]
    token_length = tokens.shape[0]
    total_length = token_length * lax.axis_size("seq")
    query_group_width = QUERY_HEADS // KEY_VALUE_HEADS
    width = conv_taps.shape[0]
    token_positions = lax.axis_index("seq") * token_length + jnp.arange(
        token_length, dtype=jnp.int32
    )
    tokens_f = tokens.astype(jnp.float32)
    normalized_rows = rms_norm(tokens_f, gain_in_f.astype(jnp.float32)).astype(jnp.bfloat16)
    query_rotated = rotary_embedding(
        matrix_product(normalized_rows, query_w).reshape(token_length, QUERY_HEADS, HEAD_SIZE),
        token_positions,
    ).astype(jnp.bfloat16)
    key_rotated = rotary_embedding(
        matrix_product(normalized_rows, key_weight_full).reshape(
            token_length, KEY_VALUE_HEADS, HEAD_SIZE
        ),
        token_positions,
    ).astype(jnp.bfloat16)
    value_low = matrix_product(normalized_rows, value_w).astype(jnp.bfloat16)
    far, (query_rotated, key_rotated, value_low, normalized_rows) = together(
        far, query_rotated, key_rotated, value_low, normalized_rows
    )
    far = further(far, steps - 3, steps - 2)
    pair_rows = along_seq(
        jnp.concatenate([key_rotated.reshape(token_length, pair_width), value_low], axis=1)
    ).reshape(total_length, 2 * pair_width)
    key_full_rows = pair_rows[:, :pair_width]
    value_full_rows = pair_rows[:, pair_width:]
    query_grouped = query_rotated.reshape(
        token_length, KEY_VALUE_HEADS, query_group_width, HEAD_SIZE
    )
    key_grouped = key_full_rows.reshape(total_length, KEY_VALUE_HEADS, HEAD_SIZE)
    value_grouped = value_full_rows.reshape(total_length, KEY_VALUE_HEADS, HEAD_SIZE)
    scores = attention_scores(query_grouped, key_grouped, token_positions, total_length)
    row_max = jnp.max(scores, axis=-1, keepdims=True)
    expo_rows = jnp.exp(scores - row_max)
    row_total = jnp.sum(expo_rows, axis=-1, keepdims=True)
    log_total = row_max + jnp.log(row_total)
    soft_low = (expo_rows / row_total).astype(jnp.bfloat16)
    attended = (
        jnp.einsum("grqk,kgd->qgrd", soft_low, value_grouped, preferred_element_type=jnp.float32)
        .reshape(token_length, QUERY_HEADS * HEAD_SIZE)
        .astype(jnp.bfloat16)
    )
    far, (attended, normalized_rows, log_total) = together(
        far, attended, normalized_rows, log_total
    )
    far = further(far, steps - 2, steps - 1)
    zgate_rows = matrix_product(normalized_rows, zgate_w)
    inner_rows = matrix_product(normalized_rows, inner_w)
    step_raw = matrix_product(normalized_rows, step_w)
    rim_rows = passed_along(inner_rows[token_length - (width - 1) :], "seq", 1)
    padded = jnp.concatenate([rim_rows, inner_rows], axis=0)
    x_heads, b_rows, c_rows, step_size, cumulative = conv_piece(
        padded, step_raw, taps_full.astype(jnp.float32), cbias_full.astype(jnp.float32), head_params
    )
    local_state, total_decay = state_piece(x_heads, b_rows, step_size, cumulative)
    far, (x_heads, b_rows, c_rows, step_size, cumulative, local_state, zgate_rows) = together(
        far, x_heads, b_rows, c_rows, step_size, cumulative, local_state, zgate_rows
    )
    far = further(far, steps - 1, steps)
    decay_in, state_in = prefix(
        (total_decay, local_state),
        "seq",
        chain_combine,
        (jnp.ones_like(total_decay), jnp.zeros_like(local_state)),
    )
    mixed_norm = output_piece(
        x_heads,
        b_rows,
        c_rows,
        step_size,
        cumulative,
        state_in,
        zgate_rows,
        ssm_gain_f.astype(jnp.float32),
        head_params,
    )
    mixed_low = mixed_norm.astype(jnp.bfloat16)
    far, (mixed_low,) = together(far, mixed_low)
    branch_w, gate_w, up_w, down_w = [
        block.reshape(count * shard_rows, block.shape[-1]) for block in far
    ]
    output_w = branch_w[:, : w_output.shape[1]]
    mixout_w = branch_w[:, w_output.shape[1] :]
    attn_rows = product_back(attended, output_w)
    mix_rows = product_back(mixed_low, mixout_w)
    hidden = tokens_f + attn_rows + mix_rows
    normed_mlp = rms_norm(hidden, gain_mlp_f.astype(jnp.float32)).astype(jnp.bfloat16)
    gate_rows = matrix_product(normed_mlp, gate_w)
    up_rows = matrix_product(normed_mlp, up_w)
    act_rows = swiglu(gate_rows, up_rows).astype(jnp.bfloat16)
    output = (hidden + product_back(act_rows, down_w)).astype(jnp.bfloat16)
    grad_act = matrix_product(cotangent, down_w)
    grad_wdown = product_outer(cotangent, act_rows)
    _, swiglu_pull = jax.vjp(swiglu, gate_rows, up_rows)
    grad_gate_f, grad_up_f = swiglu_pull(grad_act)
    grad_gate = grad_gate_f.astype(jnp.bfloat16)
    grad_up = grad_up_f.astype(jnp.bfloat16)
    grad_normed_mlp = product_back(grad_gate, gate_w) + product_back(grad_up, up_w)
    grad_wgate = product_outer(normed_mlp, grad_gate)
    grad_wup = product_outer(normed_mlp, grad_up)
    grad_hidden_norm, grad_gain_mlp_rows = norm_back(
        hidden, gain_mlp_f.astype(jnp.float32), grad_normed_mlp
    )
    grad_hidden = cotangent.astype(jnp.float32) + grad_hidden_norm
    branch_gradient = grad_hidden.astype(jnp.bfloat16)
    grad_wout = product_outer(branch_gradient, attended)
    grad_wmixout = product_outer(branch_gradient, mixed_low)
    early = [
        opened(total)
        for total in (
            jnp.concatenate([grad_wout, grad_wmixout], axis=1),
            grad_wgate,
            grad_wup,
            grad_wdown,
        )
    ]
    early, (branch_gradient,) = together(early, branch_gradient)
    early = narrowed_all(early, turns, 0, 1)
    grad_mixed = matrix_product(branch_gradient, mixout_w)
    grad_attended = (
        matrix_product(branch_gradient, output_w)
        .astype(jnp.bfloat16)
        .reshape(token_length, KEY_VALUE_HEADS, query_group_width, HEAD_SIZE)
    )
    scores_again = attention_scores(query_grouped, key_grouped, token_positions, total_length)
    soft_rows = jnp.exp(scores_again - log_total)
    soft_again = soft_rows.astype(jnp.bfloat16)
    grad_soft = jnp.einsum(
        "qgrd,kgd->grqk", grad_attended, value_grouped, preferred_element_type=jnp.float32
    )
    gradient_value_full = jnp.einsum(
        "grqk,qgrd->kgd", soft_again, grad_attended, preferred_element_type=jnp.float32
    )
    row_delta = jnp.sum(soft_rows * grad_soft, axis=-1, keepdims=True)
    grad_scores = (soft_rows * (grad_soft - row_delta)).astype(jnp.bfloat16)
    grad_query_rot = jnp.einsum(
        "grqk,kgd->qgrd", grad_scores, key_grouped, preferred_element_type=jnp.float32
    ) * HEAD_SIZE ** (-0.5)
    gradient_key_full = jnp.einsum(
        "grqk,qgrd->kgd", grad_scores, query_grouped, preferred_element_type=jnp.float32
    ) * HEAD_SIZE ** (-0.5)
    gradient_key_rotated, grad_value_f = (
        lax.psum_scatter(
            gradient_key_full.reshape(total_length, KEY_VALUE_HEADS * HEAD_SIZE).astype(
                jnp.bfloat16
            ),
            "seq",
            scatter_dimension=0,
            tiled=True,
        ).astype(jnp.float32),
        lax.psum_scatter(
            gradient_value_full.reshape(total_length, KEY_VALUE_HEADS * HEAD_SIZE).astype(
                jnp.bfloat16
            ),
            "seq",
            scatter_dimension=0,
            tiled=True,
        ).astype(jnp.float32),
    )
    grad_query = (
        rotary_embedding_pullback(
            grad_query_rot.reshape(token_length, QUERY_HEADS, HEAD_SIZE), token_positions
        )
        .reshape(token_length, QUERY_HEADS * HEAD_SIZE)
        .astype(jnp.bfloat16)
    )
    grad_key = (
        rotary_embedding_pullback(
            gradient_key_rotated.reshape(token_length, KEY_VALUE_HEADS, HEAD_SIZE), token_positions
        )
        .reshape(token_length, KEY_VALUE_HEADS * HEAD_SIZE)
        .astype(jnp.bfloat16)
    )
    grad_value = grad_value_f.astype(jnp.bfloat16)
    early, (grad_query, grad_key, grad_value, grad_mixed) = together(
        early, grad_query, grad_key, grad_value, grad_mixed
    )
    early = narrowed_all(early, turns, 1, 2)
    heads_total = opened(
        product_outer(
            normalized_rows, jnp.concatenate([grad_query, grad_key, grad_value], axis=1)
        )
    )
    heads_total = narrowed(heads_total, 2, 0)
    _, output_pull = jax.vjp(
        output_piece,
        x_heads,
        b_rows,
        c_rows,
        step_size,
        cumulative,
        state_in,
        zgate_rows,
        ssm_gain_f.astype(jnp.float32),
        head_params,
    )
    out_x, out_b, out_c, out_step, out_cum, out_state, out_zgate, grad_ssm_gain_rows, out_head = (
        output_pull(grad_mixed)
    )
    (early, heads_total), (out_x, out_b, out_c, out_step, out_cum, out_state, out_zgate) = together(
        (early, heads_total), out_x, out_b, out_c, out_step, out_cum, out_state, out_zgate
    )
    early = narrowed_all(early, turns, 2, steps - 1)
    heads_total = narrowed(heads_total, 2, 1)
    grad_zgate_low = out_zgate.astype(jnp.bfloat16)
    zgate_total = narrowed(opened(product_outer(normalized_rows, grad_zgate_low)), 1, 0)
    decay_after, state_grad = prefix_2(
        (total_decay, out_state),
        "seq",
        back_combine,
        (jnp.ones_like(total_decay), jnp.zeros_like(out_state)),
    )
    grad_decay = jnp.sum(state_grad * state_in, axis=(1, 2))
    _, state_pull = jax.vjp(state_piece, x_heads, b_rows, step_size, cumulative)
    state_x, state_b, state_step, state_cum = state_pull((state_grad, grad_decay))
    _, conv_pull = jax.vjp(
        conv_piece,
        padded,
        step_raw,
        taps_full.astype(jnp.float32),
        cbias_full.astype(jnp.float32),
        head_params,
    )
    grad_padded, grad_step_raw, grad_taps, grad_cbias, conv_head = conv_pull(
        (out_x + state_x, out_b + state_b, out_c, out_step + state_step, out_cum + state_cum)
    )
    (early, heads_total, zgate_total), (grad_padded, grad_step_raw) = together(
        (early, heads_total, zgate_total), grad_padded, grad_step_raw
    )
    early = narrowed_all(early, turns, steps - 1, steps)
    shard_branch, shard_wgate, shard_wup, shard_wdown = early
    shard_heads = narrowed_all([heads_total], [2], 2, steps)[0]
    shard_wzgate = narrowed_all([zgate_total], [1], 1, steps)[0]
    rim_back = passed_along(grad_padded[: width - 1], "seq", -1)
    grad_inner = grad_padded[width - 1 :] + jnp.concatenate(
        [jnp.zeros((token_length - (width - 1), grad_padded.shape[1]), jnp.float32), rim_back],
        axis=0,
    )
    grad_inner_low = grad_inner.astype(jnp.bfloat16)
    grad_step_low = grad_step_raw.astype(jnp.bfloat16)
    grad_normed = (
        product_back(grad_query, query_w)
        + product_back(grad_key, key_weight_full)
        + product_back(grad_value, value_w)
        + product_back(grad_zgate_low, zgate_w)
        + product_back(grad_inner_low, inner_w)
        + product_back(grad_step_low, step_w)
    )
    grad_winner = product_outer(normalized_rows, grad_inner_low)
    third = w_inner.shape[1] // 384 * 128
    shard_winner = [
        reduced(grad_winner[:, :third], 0),
        reduced(grad_winner[:, third : 2 * third], 1),
        reduced(grad_winner[:, 2 * third :], 2),
    ]
    grad_wstep = product_outer(normalized_rows, grad_step_low)
    grad_tokens_norm, grad_gain_in_rows = norm_back(
        tokens_f, gain_in_f.astype(jnp.float32), grad_normed
    )
    grad_tokens = (grad_hidden + grad_tokens_norm).astype(jnp.bfloat16)
    taps_by_owner = grad_taps.reshape(len(conv_taps), count, -1).transpose(1, 0, 2)
    by_owner = [taps_by_owner.reshape(count, -1)] + [
        vector.reshape(count, -1)
        for vector in (grad_cbias, grad_ssm_gain_rows, grad_gain_in_rows, grad_gain_mlp_rows)
    ]
    by_owner.append(jnp.zeros((count, spare), jnp.float32))
    shard_small = reduced(
        jnp.concatenate(
            [
                grad_wstep,
                jnp.concatenate(by_owner, axis=1).reshape(count * shard_rows, extra),
                jnp.zeros((count * shard_rows, margin), jnp.float32),
            ],
            axis=1,
        ),
        0,
    )
    shard_flat = shard_small[:, H : H + extra].reshape(-1)
    shard_vectors = [
        shard_flat[edges[i] : edges[i + 1]].reshape(vectors[i].shape) for i in range(len(vectors))
    ]
    grad_head = summed(out_head + conv_head)
    return (
        output,
        grad_tokens,
        shard_vectors[3],
        shard_heads[:, :heads_width],
        shard_heads[:, heads_width : heads_width + pair_width],
        shard_heads[:, heads_width + pair_width :],
        shard_branch[:, : w_output.shape[1]],
        shard_wzgate,
        jnp.concatenate(shard_winner, axis=1),
        shard_small[:, :H],
        shard_vectors[0],
        shard_vectors[1],
        shard_vectors[2],
        shard_branch[:, w_output.shape[1] :],
        shard_vectors[4],
        shard_wgate,
        shard_wup,
        shard_wdown,
        grad_head,
    )


def solution(mesh):
    return jax.shard_map(
        shards,
        mesh=mesh,
        in_specs=(
            P(("dp", "seq"), None),
            P(("dp", "seq")),
            P(("dp", "seq"), None),
            P(("dp", "seq"), None),
            P(("dp", "seq"), None),
            P(("dp", "seq"), None),
            P(("dp", "seq"), None),
            P(("dp", "seq"), None),
            P(("dp", "seq"), None),
            P(None, ("dp", "seq")),
            P(("dp", "seq")),
            P(("dp", "seq")),
            P(("dp", "seq"), None),
            P(("dp", "seq")),
            P(("dp", "seq"), None),
            P(("dp", "seq"), None),
            P(("dp", "seq"), None),
            P(),
            P(("dp", "seq"), None),
        ),
        out_specs=(
            P(("dp", "seq"), None),
            P(("dp", "seq"), None),
            P(("dp", "seq")),
            P(("dp", "seq"), None),
            P(("dp", "seq"), None),
            P(("dp", "seq"), None),
            P(("dp", "seq"), None),
            P(("dp", "seq"), None),
            P(("dp", "seq"), None),
            P(("dp", "seq"), None),
            P(None, ("dp", "seq")),
            P(("dp", "seq")),
            P(("dp", "seq")),
            P(("dp", "seq"), None),
            P(("dp", "seq")),
            P(("dp", "seq"), None),
            P(("dp", "seq"), None),
            P(("dp", "seq"), None),
            P(),
        ),
        check_vma=False,
    )
```
